512 devices in a mesh: vox: 64 (over y, z_lo, core), mode: 8 (over z_hi, x).
Axes of the slice: x: 4, y: 4, z: 16 (z_hi: 2, z_lo: 8; z = z_hi * 8 + z_lo), core: 2. Of those that a mesh axis runs over, the one named last changes fastest.
Arguments:
- modes_in: bfloat16 [128, 3, 64, 32, 128], P('mode', None, 'vox'), may hold values from -6 to 6
- class_map: int32 [64, 32, 128], P('vox'), may hold values from 0 to 7
- stiffness_table: float32 [8], replicated, may hold values from 0.5 to 2
- coefficients: float32 [128, 128], replicated, may hold values from -0.5 to 0.5
Outputs:
- modes_out: bfloat16 [128, 3, 64, 32, 128], P('mode', None, 'vox')
The draws below stay inside these ranges and needn't reach their ends.
Inputs may be any that keep to these rules, and one draw needn't show every extreme that they name: `class_map`: class numbers index the stiffness table.
All inputs are finite; a program needn't handle non-finite values.
Results may differ from the reference program's by a relative error of at most 0.0081.
Values may be sent and summed in bfloat16 or wider, within the bound.
A program may use at most 64 MiB of HBM per device.

```python
import math
import jax
import jax.numpy as jnp
from jax import lax

MODES = 128
COMP = 3
NCLASS = 8
DEGREE = 3
NX = 32
NY = 128
NZ = 64
VOXELS = 262144


shared_count = 8


layer_low = 0.3


layer_high = 2.4


pi_value = 3.14159265


def phase_planes(key, x_frac, y_frac):
    key_weight, key_comp, key_wavex, key_wavey = jax.random.split(key, 4)
    wave_x = jax.random.randint(key_wavex, (shared_count,), 1, 4).astype(jnp.float32)
    wave_y = jax.random.randint(key_wavey, (shared_count,), 1, 4).astype(jnp.float32)
    comp_weight = jax.random.normal(key_comp, (shared_count, COMP), jnp.float32)
    mode_weight = jax.random.normal(key_weight, (MODES, shared_count), jnp.float32) * jnp.float32(0.35355339)
    planes_sum = jnp.zeros((MODES, COMP, NX, NY), jnp.float32)
    for member in range(shared_count):
        plane_term = jnp.sin(pi_value * wave_x[member] * x_frac)[:, None] * jnp.sin(pi_value * wave_y[member] * y_frac)[None, :]
        planes_sum = planes_sum + mode_weight[:, member, None, None, None] * comp_weight[member][None, :, None, None] * plane_term[None, None]
    return planes_sum


def draw_modes_in(key, part):
    key = jax.random.fold_in(key, 11)
    key_own, key_cos, key_sin, key_size, key_layer = jax.random.split(key, 5)
    field_shape = (COMP, NZ, NX, NY)
    own_field = jax.random.normal(key_own, (MODES,) + field_shape, jnp.float32)
    own_part = 0.6
    size_low = 0.3
    size_high = 1.2
    x_frac = (jnp.arange(NX, dtype=jnp.float32) + 1.0) / jnp.float32(NX + 1.0)
    y_frac = (jnp.arange(NY, dtype=jnp.float32) + 1.0) / jnp.float32(NY + 1.0)
    z_angle = jnp.arange(NZ, dtype=jnp.float32) * jnp.float32(0.5 * pi_value)
    cos_planes = phase_planes(key_cos, x_frac, y_frac)
    sin_planes = phase_planes(key_sin, x_frac, y_frac)
    mode_size = jnp.exp(jax.random.uniform(key_size, (MODES,), jnp.float32, jnp.log(size_low), jnp.log(size_high)))
    pattern = cos_planes[:, :, None] * jnp.cos(z_angle)[None, None, :, None, None] + sin_planes[:, :, None] * jnp.sin(z_angle)[None, None, :, None, None]
    layer_log = jax.random.uniform(key_layer, (NZ,), jnp.float32, jnp.log(layer_low), jnp.log(layer_high))
    layer_scale = jnp.exp(layer_log)
    values = (own_part * own_field + mode_size[:, None, None, None, None] * pattern) * layer_scale[None, None, :, None, None]
    return jnp.clip(values, -6.0, 6.0).astype(jnp.bfloat16)


def set_ends(values, own_key, low, largest):
    extent = values.shape
    spot = [jax.random.randint(jax.random.fold_in(own_key, axis), (), 0, extent[axis]) for axis in range(len(extent))]
    values = values.at[tuple(spot)].set(low)
    longest = extent.index(max(extent))
    spot[longest] = (spot[longest] + 1) % extent[longest]
    return values.at[tuple(spot)].set(largest)


def normal_values(rng, shape, scale, bound, held_as=jnp.bfloat16):
    values = scale * jax.random.normal(rng, shape, jnp.float32)
    return jnp.clip(values, min=-bound, max=bound).astype(held_as)


def setup_inputs(seed: int = 0) -> dict:
    splits = jax.random.split(jax.random.key(seed), 5)
    return {
        "modes_in": draw_modes_in(jax.random.fold_in(splits[4], 71), 0),
        "class_map": set_ends(jax.random.randint(splits[1], (NZ, NX, NY), 0, NCLASS), jax.random.fold_in(splits[1], 1), 0, NCLASS - 1).astype(jnp.int32),
        "stiffness_table": jnp.clip(jnp.exp(jax.random.uniform(splits[2], (NCLASS,), jnp.float32, math.log(0.5), math.log(2.0))), 0.5, 2.0),
        "coefficients": normal_values(splits[3], (MODES, MODES), MODES ** -0.5, 0.5, jnp.float32),
    }


def offset_list():
    found = []
    for dz in (-1, 0, 1):
        for dx in (-1, 0, 1):
            for dy in (-1, 0, 1):
                count = abs(dz) + abs(dx) + abs(dy)
                if count > 0:
                    found.append((dz, dx, dy, [0.0, 1.0, 0.5, 0.25][count]))
    return found

def pad_grid(field):
    lead = field.ndim - 3
    wrapped = jnp.pad(field, [(0, 0)] * lead + [(1, 1), (0, 0), (0, 0)], mode='wrap')
    return jnp.pad(wrapped, [(0, 0)] * lead + [(0, 0), (1, 1), (1, 1)])

def shifted(padded, dz, dx, dy, zlen, xlen, ylen):
    return padded[..., 1 + dz:1 + dz + zlen, 1 + dx:1 + dx + xlen, 1 + dy:1 + dy + ylen]

def reference(modes_in, class_map, stiffness_table, coefficients):
    classes = jnp.arange(NCLASS, dtype=jnp.int32)
    stiff = lax.optimization_barrier(jnp.sum(jnp.where(class_map[None] == classes[:, None, None, None], stiffness_table[:, None, None, None], jnp.float32(0.0)), axis=0))
    spad = pad_grid(stiff)
    zlen, xlen, ylen = stiff.shape
    terms = []
    for dz, dx, dy, weight in offset_list():
        terms.append((dz, dx, dy, weight * 0.5 * (stiff + shifted(spad, dz, dx, dy, zlen, xlen, ylen))))

    def apply_op(field):
        padded = pad_grid(field)
        total = jnp.zeros_like(field)
        for dz, dx, dy, kedge in terms:
            total = total + kedge * (field - shifted(padded, dz, dx, dy, zlen, xlen, ylen))
        return total

    def filter_one(column):
        scale_e = jnp.float32(21.0)
        centre = jnp.float32(35.0)
        older = column.astype(jnp.float32)
        newer = (apply_op(older) - centre * older) / scale_e
        for step in range(DEGREE - 1):
            nxt = 2.0 * (apply_op(newer) - centre * newer) / scale_e - older
            older, newer = (newer, nxt)
        return newer.astype(jnp.bfloat16)
    filtered = lax.map(filter_one, modes_in)
    flat = filtered.reshape(MODES, -1)
    gram = jnp.dot(flat.astype(jnp.float32), flat.T.astype(jnp.float32), preferred_element_type=jnp.float32)
    lower = jnp.linalg.cholesky(gram)
    total_rows = COMP * VOXELS
    solved = lax.linalg.triangular_solve(lower, coefficients, left_side=True, lower=True, transpose_a=True)
    mix = (solved * jnp.sqrt(jnp.float32(total_rows))).astype(jnp.bfloat16)
    result = jnp.dot(mix.T.astype(jnp.float32), flat.astype(jnp.float32), preferred_element_type=jnp.float32).astype(jnp.bfloat16)
    return result.reshape(modes_in.shape)
```

```python
import functools

import jax
import jax.numpy as jnp
from jax import lax
from jax.experimental import pallas as pl
from jax.experimental.pallas import tpu as pltpu
from jax.sharding import PartitionSpec as P

MESH = pl.DeviceIdType.MESH
F32 = jnp.float32
BF16 = jnp.bfloat16
E = 21.0
CENTRE = 35.0


class Sizes:
    def __init__(self, y, z_lo, z_hi, x, own=16, comps=3, nx=32, ny=128):
        self.y, self.z_lo, self.z_hi, self.x = y, z_lo, z_hi, x
        self.vox = y * z_lo * 2
        self.mode = z_hi * x
        self.own, self.comps, self.nx, self.ny = own, comps, nx, ny
        self.modes = self.mode * own
        self.rows = nx // x
        self.half = self.rows // z_hi
        self.group = x * y * 2
        self.zs = z_hi * z_lo
        self.piece = self.modes // self.group


class Place:
    def __init__(self, n):
        self.n = n
        self.v = lax.axis_index("vox")
        self.m = lax.axis_index("mode")
        self.y = lax.div(self.v, n.z_lo * 2)
        self.zl = lax.rem(lax.div(self.v, 2), n.z_lo)
        self.c = lax.rem(self.v, 2)
        self.zh = lax.div(self.m, n.x)
        self.x = lax.rem(self.m, n.x)
        self.g = (self.x * n.y + self.y) * 2 + self.c
        self.z = self.zh * n.z_lo + self.zl

    def in_group(self, g):
        n = self.n
        c, y, x = lax.rem(g, 2), lax.rem(lax.div(g, 2), n.y), lax.div(g, 2 * n.y)
        return {"vox": (y * n.z_lo + self.zl) * 2 + c, "mode": self.zh * n.x + x}

    def in_column(self, z):
        n = self.n
        zl, zh = lax.rem(z, n.z_lo), lax.div(z, n.z_lo)
        return {"vox": (self.y * n.z_lo + zl) * 2 + self.c, "mode": zh * n.x + self.x}


def remote(src, dst, send, recv, device):
    return pltpu.make_async_remote_copy(
        src_ref=src, dst_ref=dst, send_sem=send, recv_sem=recv,
        device_id=device, device_id_type=MESH,
    )


def meet(devices):
    barrier = pltpu.get_barrier_semaphore()
    for device in devices:
        pl.semaphore_signal(barrier, inc=1, device_id=device, device_id_type=MESH)
    pl.semaphore_wait(barrier, len(devices))


def filter_kernel(
    n, y0, cls, table, out_r,
    halo, shalo, sown, sm, sh, sp, dd, y1, y2, y1b, y2b, filt,
    hsend, hrecv, ssend, srecv, asend, arecv,
):
    me = Place(n)
    nxt = {"vox": lax.rem(me.v + 1, n.vox)}
    prv = {"vox": lax.rem(me.v + n.vox - 1, n.vox)}
    mates = [{"mode": lax.rem(me.m + d, n.mode)} for d in range(1, n.mode)]
    meet([nxt, prv] + mates)

    planes = cls[...]
    s = jnp.zeros((n.nx, n.ny), F32)
    for k in range(table.shape[0]):
        s = s + jnp.where(planes == k, table[k], 0.0)
    sown[...] = s
    scopies = [
        remote(sown, shalo.at[d], ssend.at[d], srecv.at[d], (nxt, prv)[d]) for d in range(2)
    ]
    for copy in scopies:
        copy.start()

    def hop(r, c, d):
        src = (y0, y1b, y2b)[r]
        return remote(
            src.at[c], halo.at[r, d, c], hsend.at[r, d, c], hrecv.at[r, d, c], (nxt, prv)[d]
        )

    for c in range(n.comps):
        for d in range(2):
            hop(0, c, d).start()

    lane = lax.broadcasted_iota(jnp.int32, (n.own, n.ny), 1)
    first, last = lane == 0, lane == n.ny - 1

    def along_y(u):
        before = jnp.where(first, 0.0, pltpu.roll(u, 1, 1))
        after = jnp.where(last, 0.0, pltpu.roll(u, n.ny - 1, 1))
        return (before + after) + (u + u)

    for copy in scopies:
        copy.wait()
    below, above = shalo[0], shalo[1]
    layers = below + above + (s + s)
    col = lax.broadcasted_iota(jnp.int32, (n.nx, n.ny), 1)
    row = lax.broadcasted_iota(jnp.int32, (n.nx, n.ny), 0)
    ty = (
        jnp.where(col == 0, 0.0, pltpu.roll(layers, 1, 1))
        + jnp.where(col == n.ny - 1, 0.0, pltpu.roll(layers, n.ny - 1, 1))
        + (layers + layers)
    )
    txy = (
        jnp.where(row == 0, 0.0, pltpu.roll(ty, 1, 0))
        + jnp.where(row == n.nx - 1, 0.0, pltpu.roll(ty, n.nx - 1, 0))
        + (ty + ty)
    )
    diag = (8.0 * s + 0.125 * txy - CENTRE) * (1.0 / E)
    part = 1.0 / (8.0 * E)
    for x in range(n.nx):
        wide = lambda a: jnp.broadcast_to(a[x : x + 1, :], (n.own, n.ny))
        sm[x] = wide(below * part)
        sh[x] = wide(s * (2.0 * part))
        sp[x] = wide(above * part)
        dd[x] = wide(diag)

    def stencil(r, c):
        def centre(x):
            if r == 0:
                return y0[c, x].astype(F32)
            return (y1, y2)[r - 1][c, x]

        def layer_sums(x):
            lo, mid, hi = halo[r, 0, c, x].astype(F32), centre(x), halo[r, 1, c, x].astype(F32)
            plain = (lo + hi) * 0.5 + mid
            weighted = sm[x] * lo + sh[x] * mid + sp[x] * hi
            return along_y(plain), along_y(weighted)

        def finish(x, a, b):
            value = dd[x] * centre(x) - (sh[x] * a + b)
            if r == 0:
                y1[c, x] = value
                y1b[c, x] = value.astype(BF16)
            elif r == 1:
                value = (value + value) - y0[c, x].astype(F32)
                y2[c, x] = value
                y2b[c, x] = value.astype(BF16)
            else:
                filt[c, x] = ((value + value) - y1[c, x]).astype(BF16)

        def body(x, carry):
            a0, a1, b0, b1 = carry
            a2, b2 = layer_sums(x + 1)
            finish(x, (a0 + a2) + (a1 + a1), (b0 + b2) + (b1 + b1))
            return a1, a2, b1, b2

        zero = jnp.zeros((n.own, n.ny), F32)
        a, b = layer_sums(0)
        a0, a1, b0, b1 = lax.fori_loop(0, n.nx - 1, body, (zero, a, zero, b))
        finish(n.nx - 1, a0 + (a1 + a1), b0 + (b1 + b1))

    def share(c, d, part):
        to = lax.rem(me.m + d, n.mode)
        to_x, to_zh = lax.rem(to, n.x), lax.div(to, n.x)
        at = lax.rem(to_zh + part, n.z_hi) * n.half
        src = filt.at[c, pl.ds(to_x * n.rows + at, n.half)]
        dst = out_r.at[c, pl.ds(at, n.half), pl.ds(pl.multiple_of(me.m * n.own, n.own), n.own)]
        return remote(src, dst, asend.at[part, c, d], arecv.at[part, c, d], {"mode": to})

    for r in range(3):
        for c in range(n.comps):
            for d in range(2):
                hop(r, c, d).wait_recv()
            stencil(r, c)
            if r < 2:
                for d in range(2):
                    hop(r + 1, c, d).start()
            else:
                for d in range(1, n.mode):
                    share(c, d, 0).start()
    for c in range(n.comps):
        for d in range(1, n.mode):
            share(c, d, 1).start()
        out_r[c, :, pl.ds(pl.multiple_of(me.m * n.own, n.own), n.own), :] = filt[
            c, pl.ds(me.x * n.rows, n.rows)
        ]
    for part in range(2):
        for c in range(n.comps):
            for d in range(1, n.mode):
                share(c, d, part).wait()
    for r in range(3):
        for c in range(n.comps):
            for d in range(2):
                hop(r, c, d).wait_send()


def run_filter(n, y0, cls, table):
    plane = (n.comps, n.nx, n.own, n.ny)
    vmem = pl.BlockSpec(memory_space=pltpu.VMEM)
    return pl.pallas_call(
        functools.partial(filter_kernel, n),
        out_shape=jax.ShapeDtypeStruct((n.comps, n.rows, n.modes, n.ny), BF16),
        in_specs=[vmem, vmem, pl.BlockSpec(memory_space=pltpu.SMEM)],
        out_specs=vmem,
        scratch_shapes=[
            pltpu.VMEM((3, 2) + plane, BF16),
            pltpu.VMEM((2, n.nx, n.ny), F32),
            pltpu.VMEM((n.nx, n.ny), F32),
        ]
        + [pltpu.VMEM((n.nx, n.own, n.ny), F32)] * 4
        + [pltpu.VMEM(plane, F32)] * 2
        + [pltpu.VMEM(plane, BF16)] * 3
        + [
            pltpu.SemaphoreType.DMA((3, 2, n.comps)),
            pltpu.SemaphoreType.DMA((3, 2, n.comps)),
            pltpu.SemaphoreType.DMA((2,)),
            pltpu.SemaphoreType.DMA((2,)),
            pltpu.SemaphoreType.DMA((2, n.comps, n.mode)),
            pltpu.SemaphoreType.DMA((2, n.comps, n.mode)),
        ],
        compiler_params=pltpu.CompilerParams(
            collective_id=1, has_side_effects=True, vmem_limit_bytes=40 << 20
        ),
        name="filter",
    )(y0, cls, table)


def gram_kernel(n, block, out, own, parts, column, total, send1, recv1, send2, recv2, send3, recv3):
    me = Place(n)
    group = [me.in_group(lax.rem(me.g + d, n.group)) for d in range(1, n.group)]
    stack = [me.in_column(lax.rem(me.z + d, n.zs)) for d in range(1, n.zs)]
    meet(group + stack)
    gram = jnp.zeros((n.modes, n.modes), F32)
    for c in range(n.comps):
        for k in range(n.half):
            a = block[c, me.zh * n.half + k]
            gram = gram + lax.dot_general(
                a, a, (((1,), (1,)), ((), ())), preferred_element_type=F32
            )
    for i in range(n.group):
        own[i] = gram[i * n.piece : (i + 1) * n.piece]

    def scatter(d):
        to = lax.rem(me.g + d, n.group)
        return remote(own.at[to], parts.at[d], send1.at[d], recv1.at[d], me.in_group(to))

    def around(d):
        to = lax.rem(me.z + d, n.zs)
        return remote(total, column.at[me.z], send2.at[d], recv2.at[d], me.in_column(to))

    def gather(d):
        to = lax.rem(me.g + d, n.group)
        return remote(total, out.at[me.g], send3.at[d], recv3.at[d], me.in_group(to))

    for d in range(1, n.group):
        scatter(d).start()
    mine = own[me.g]
    for d in range(1, n.group):
        scatter(d).wait()
        mine = mine + parts[d]
    total[...] = mine
    column[me.z] = mine
    for d in range(1, n.zs):
        around(d).start()
    for d in range(1, n.zs):
        around(d).wait()
    mine = column[0]
    for z in range(1, n.zs):
        mine = mine + column[z]
    total[...] = mine
    out[me.g] = mine
    for d in range(1, n.group):
        gather(d).start()
    for d in range(1, n.group):
        gather(d).wait()


def run_gram(n, block):
    vmem = pl.BlockSpec(memory_space=pltpu.VMEM)
    piece = (n.piece, n.modes)
    dma = pltpu.SemaphoreType.DMA
    return pl.pallas_call(
        functools.partial(gram_kernel, n),
        out_shape=jax.ShapeDtypeStruct((n.group,) + piece, F32),
        in_specs=[vmem],
        out_specs=vmem,
        scratch_shapes=[
            pltpu.VMEM((n.group,) + piece, F32),
            pltpu.VMEM((n.group,) + piece, F32),
            pltpu.VMEM((n.zs,) + piece, F32),
            pltpu.VMEM(piece, F32),
            dma((n.group,)), dma((n.group,)), dma((n.zs,)), dma((n.zs,)),
            dma((n.group,)), dma((n.group,)),
        ],
        compiler_params=pltpu.CompilerParams(
            collective_id=2, has_side_effects=True, vmem_limit_bytes=40 << 20
        ),
        name="gram",
    )(block)


def rotate_kernel(n, block, mix_t, out, held, send, recv):
    me = Place(n)
    meet([{"mode": me.zh * n.x + lax.rem(me.x + d, n.x)} for d in range(1, n.x)])
    mine = pl.ds(pl.multiple_of(me.x * n.own, n.own), n.own)

    def back(c, d):
        to = lax.rem(me.x + d, n.x)
        src = held.at[c, :, pl.ds(pl.multiple_of(to * n.own, n.own), n.own)]
        dst = out.at[c, pl.ds(me.x * n.rows, n.rows)]
        return remote(src, dst, send.at[c, d], recv.at[c, d], {"mode": me.zh * n.x + to})

    weights = mix_t[...]
    for c in range(n.comps):
        for k in range(n.rows):
            held[c, k] = jnp.dot(weights, block[c, k], preferred_element_type=F32).astype(BF16)
        for d in range(1, n.x):
            back(c, d).start()
    for c in range(n.comps):
        out[c, pl.ds(me.x * n.rows, n.rows)] = held[c, :, mine, :]
    for c in range(n.comps):
        for d in range(1, n.x):
            back(c, d).wait()


def run_rotate(n, block, mix_t):
    vmem = pl.BlockSpec(memory_space=pltpu.VMEM)
    return pl.pallas_call(
        functools.partial(rotate_kernel, n),
        out_shape=jax.ShapeDtypeStruct((n.comps, n.nx, n.own, n.ny), BF16),
        in_specs=[vmem, vmem],
        out_specs=vmem,
        scratch_shapes=[
            pltpu.VMEM((n.comps, n.rows, n.x * n.own, n.ny), BF16),
            pltpu.SemaphoreType.DMA((n.comps, n.x)),
            pltpu.SemaphoreType.DMA((n.comps, n.x)),
        ],
        compiler_params=pltpu.CompilerParams(
            collective_id=3, has_side_effects=True, vmem_limit_bytes=40 << 20
        ),
        name="rotate",
    )(block, mix_t)


def make_mix(gram, coefficients, total_rows):
    lower = jnp.linalg.cholesky(gram)
    solved = lax.linalg.triangular_solve(
        lower, coefficients, left_side=True, lower=True, transpose_a=True
    )
    return (solved * jnp.sqrt(jnp.float32(total_rows))).astype(BF16)


def per_device(n, modes_in, class_map, stiffness_table, coefficients):
    y0 = jnp.transpose(modes_in[:, :, 0], (1, 2, 0, 3))
    block = run_filter(n, y0, class_map[0], stiffness_table)
    gram = run_gram(n, block).reshape(n.modes, n.modes)
    mix = make_mix(gram, coefficients, n.comps * n.vox * n.nx * n.ny)
    width = n.x * n.own
    start = lax.div(lax.axis_index("mode"), n.x) * width
    mix_t = lax.dynamic_slice_in_dim(mix.T, start, width, 0)
    result = run_rotate(n, block, mix_t)
    return jnp.transpose(result, (2, 0, 1, 3))[:, :, None]


def build(mesh, n):
    spec = P("mode", None, "vox", None, None)
    return jax.shard_map(
        functools.partial(per_device, n), mesh=mesh,
        in_specs=(spec, P("vox", None, None), P(), P()), out_specs=spec, check_vma=False,
    )


def solution(mesh):
    return build(mesh, Sizes(y=4, z_lo=8, z_hi=2, x=4))
```

```python
import functools
import math

import jax
import jax.numpy as jnp
from jax import lax
from jax.experimental import pallas as pl
from jax.experimental.pallas import tpu as pltpu
from jax.sharding import PartitionSpec as P

MESH = pl.DeviceIdType.MESH
F32 = jnp.float32
BF16 = jnp.bfloat16
E = 21.0
CENTRE = 35.0


class Sizes:
    def __init__(self, y, z_lo, z_hi, x, own=16, comps=3, nx=32, ny=128):
        self.y, self.z_lo, self.z_hi, self.x = y, z_lo, z_hi, x
        self.vox = y * z_lo * 2
        self.mode = z_hi * x
        self.own, self.comps, self.nx, self.ny = own, comps, nx, ny
        self.modes = self.mode * own
        self.rows = nx // x
        self.half = self.rows // z_hi
        self.group = x * y * 2
        self.zs = z_hi * z_lo
        self.piece = self.modes // self.group


class Place:
    def __init__(self, n):
        self.n = n
        self.v = lax.axis_index("vox")
        self.m = lax.axis_index("mode")
        self.y = lax.div(self.v, n.z_lo * 2)
        self.zl = lax.rem(lax.div(self.v, 2), n.z_lo)
        self.c = lax.rem(self.v, 2)
        self.zh = lax.div(self.m, n.x)
        self.x = lax.rem(self.m, n.x)
        self.g = (self.x * n.y + self.y) * 2 + self.c
        self.z = self.zh * n.z_lo + self.zl

    def in_group(self, dx, dy, dc):
        n = self.n
        x, y, c = lax.rem(self.x + dx, n.x), lax.rem(self.y + dy, n.y), lax.rem(self.c + dc, 2)
        device = {"vox": (y * n.z_lo + self.zl) * 2 + c, "mode": self.zh * n.x + x}
        return device, (x * n.y + y) * 2 + c

    def in_column(self, z):
        n = self.n
        zl, zh = lax.rem(z, n.z_lo), lax.div(z, n.z_lo)
        return {"vox": (self.y * n.z_lo + zl) * 2 + self.c, "mode": zh * n.x + self.x}


def remote(src, dst, send, recv, device):
    return pltpu.make_async_remote_copy(
        src_ref=src, dst_ref=dst, send_sem=send, recv_sem=recv,
        device_id=device, device_id_type=MESH,
    )


def sum_rows(a, before, after):
    return (before + after) + (a + a)


def whiten(gram, size, scale):
    row = lax.broadcasted_iota(jnp.int32, (size, size), 0)
    rest = gram
    inverse = jnp.where(row == lax.broadcasted_iota(jnp.int32, (size, size), 1), 1.0, 0.0)
    sub = row[:8]
    done = []
    for k in range(size // 8):
        left = size - 8 * k
        wide = lambda a, i: jnp.broadcast_to(a[i : i + 1], (left, size))
        cols = [
            jnp.broadcast_to(rest[:, 8 * k + j : 8 * k + j + 1], (left, size)) for j in range(8)
        ]
        root = jnp.zeros((8, size), F32)
        for i in range(8):
            pivot = cols[i][i : i + 1]
            inv = 1.0 / pivot
            factor = jnp.where(row[:left] > i, cols[i], 0.0) * jnp.broadcast_to(inv, (left, size))
            for j in range(i + 1, 8):
                cols[j] = cols[j] - factor * wide(cols[j], i)
            rest = rest - factor * wide(rest, i)
            inverse = inverse - factor * wide(inverse, i)
            root = jnp.where(sub == i, jnp.broadcast_to(lax.rsqrt(pivot) * scale, (8, size)), root)
        done.append(inverse[:8] * root)
        rest, inverse = rest[8:], inverse[8:]
    return done


def kernel(
    n, y0, cls, table, coef_t, out,
    halo, shalo, sown, sm, sh, sp, dd, y1, y2, y1b, y2b, filt, block,
    own, parts, column, total, pieces, gram, white, held,
    hsend, hrecv, ssend, srecv, asend, arecv,
    send1, recv1, send2, recv2, send3, recv3, send4, recv4,
):
    me = Place(n)
    nxt = {"vox": lax.rem(me.v + 1, n.vox)}
    prv = {"vox": lax.rem(me.v + n.vox - 1, n.vox)}
    far = lambda d, size: min(d, size - d)
    steps = [(dx, dy, dc) for dx in range(n.x) for dy in range(n.y) for dc in range(2)]
    steps = sorted(steps[1:], key=lambda s: (-far(s[0], n.x) - far(s[1], n.y), s))
    climbs = sorted(range(1, n.zs), key=lambda d: (-far(d, n.zs), d))

    barrier = pltpu.get_barrier_semaphore()
    friends = [nxt, prv]
    friends += [me.in_group(*step)[0] for step in steps]
    friends += [me.in_column(lax.rem(me.z + d, n.zs)) for d in climbs]
    for dz in range(1, n.z_hi):
        for dx in range(1, n.x):
            friends.append({
                "mode": lax.rem(me.zh + dz, n.z_hi) * n.x + lax.rem(me.x + dx, n.x)
            })
    for device in friends:
        pl.semaphore_signal(barrier, inc=1, device_id=device, device_id_type=MESH)

    planes = cls[...]
    s = jnp.zeros((n.nx, n.ny), F32)
    for k in range(table.shape[0]):
        s = s + jnp.where(planes == k, table[k], 0.0)
    sown[...] = s
    pl.semaphore_wait(barrier, len(friends))

    scopies = [
        remote(sown, shalo.at[d], ssend.at[d], srecv.at[d], (nxt, prv)[d]) for d in range(2)
    ]
    for copy in scopies:
        copy.start()

    def hop(r, c, d):
        src = (y0, y1b, y2b)[r]
        return remote(
            src.at[c], halo.at[r, d, c], hsend.at[r, d, c], hrecv.at[r, d, c], (nxt, prv)[d]
        )

    for c in range(n.comps):
        for d in range(2):
            hop(0, c, d).start()

    for copy in scopies:
        copy.wait()
    below, above = shalo[0], shalo[1]
    col = lax.broadcasted_iota(jnp.int32, (n.nx, n.ny), 1)
    row = lax.broadcasted_iota(jnp.int32, (n.nx, n.ny), 0)
    layers = sum_rows(s, below, above)
    ty = sum_rows(
        layers,
        jnp.where(col == 0, 0.0, pltpu.roll(layers, 1, 1)),
        jnp.where(col == n.ny - 1, 0.0, pltpu.roll(layers, n.ny - 1, 1)),
    )
    txy = sum_rows(
        ty,
        jnp.where(row == 0, 0.0, pltpu.roll(ty, 1, 0)),
        jnp.where(row == n.nx - 1, 0.0, pltpu.roll(ty, n.nx - 1, 0)),
    )
    diag = (8.0 * s + 0.125 * txy - CENTRE) * (1.0 / E)
    part = 1.0 / (8.0 * E)
    for held_in, values in ((sm, below * part), (sh, s * (2.0 * part)), (sp, above * part), (dd, diag)):
        for x in range(n.nx):
            held_in[x] = jnp.broadcast_to(values[x : x + 1, :], (n.own, n.ny))

    strip = 4
    lane = lax.broadcasted_iota(jnp.int32, (n.own, n.ny), 1)
    first, last = lane == 0, lane == n.ny - 1

    def along_y(u):
        rows = []
        for i in range(u.shape[0]):
            v = u[i]
            before = jnp.where(first, 0.0, pltpu.roll(v, 1, 1))
            after = jnp.where(last, 0.0, pltpu.roll(v, n.ny - 1, 1))
            rows.append(sum_rows(v, before, after))
        return jnp.stack(rows)

    def stencil(r, c):
        def centre(at):
            if r == 0:
                return y0[c, at].astype(F32)
            return (y1, y2)[r - 1][c, at]

        def layer_sums(lo_row, hi_row):
            at = slice(lo_row, hi_row)
            lo, mid, hi = halo[r, 0, c, at].astype(F32), centre(at), halo[r, 1, c, at].astype(F32)
            plain = (lo + hi) * 0.5 + mid
            weighted = sm[at] * lo + sh[at] * mid + sp[at] * hi
            return along_y(plain), along_y(weighted)

        zero = jnp.zeros((1, n.own, n.ny), F32)
        a, b = layer_sums(0, 1)
        a, b = jnp.concatenate([zero, a]), jnp.concatenate([zero, b])
        for x in range(0, n.nx, strip):
            at = slice(x, x + strip)
            more = list(layer_sums(x + 1, min(x + strip + 1, n.nx)))
            if x + strip == n.nx:
                more = [jnp.concatenate([u, zero]) for u in more]
            a, b = jnp.concatenate([a, more[0]]), jnp.concatenate([b, more[1]])
            fold = lambda u: sum_rows(u[1 : strip + 1], u[:strip], u[2:])
            value = dd[at] * centre(at) - (sh[at] * fold(a) + fold(b))
            a, b = a[strip:], b[strip:]
            if r == 0:
                y1[c, at] = value
                y1b[c, at] = value.astype(BF16)
            elif r == 1:
                value = (value + value) - y0[c, at].astype(F32)
                y2[c, at] = value
                y2b[c, at] = value.astype(BF16)
            else:
                filt[c, at] = ((value + value) - y1[c, at]).astype(BF16)

    mine = pl.ds(pl.multiple_of(me.m * n.own, n.own), n.own)

    def share(c, d, part):
        to = lax.rem(me.m + d, n.mode)
        to_x, to_zh = lax.rem(to, n.x), lax.div(to, n.x)
        at = lax.rem(to_zh + part, n.z_hi) * n.half
        src = filt.at[c, pl.ds(to_x * n.rows + at, n.half)]
        dst = block.at[c, pl.ds(at, n.half), mine]
        return remote(src, dst, asend.at[part, c, d], arecv.at[part, c, d], {"mode": to})

    shares = range(1, n.mode)
    for r in range(3):
        for c in range(n.comps):
            for d in range(2):
                hop(r, c, d).wait_recv()
            stencil(r, c)
            if r < 2:
                for d in range(2):
                    hop(r + 1, c, d).start()
            else:
                for d in shares:
                    share(c, d, 0).start()
                block[c, :, mine, :] = filt[c, pl.ds(me.x * n.rows, n.rows)]
    for d in shares:
        share(0, d, 1).start()

    product = jnp.zeros((n.modes, n.modes), F32)
    for c in range(n.comps):
        for d in shares:
            share(c, d, 0).wait_recv()
        for k in range(n.half):
            a = block[c, me.zh * n.half + k]
            product = product + lax.dot_general(
                a, a, (((1,), (1,)), ((), ())), preferred_element_type=F32
            )
    for i in range(n.group):
        own[i] = product[i * n.piece : (i + 1) * n.piece]

    def scatter(i):
        device, to = me.in_group(*steps[i])
        return remote(own.at[to], parts.at[i], send1.at[i], recv1.at[i], device)

    def around(d):
        to = me.in_column(lax.rem(me.z + d, n.zs))
        return remote(total, column.at[me.z], send2.at[d], recv2.at[d], to)

    def gather(i):
        device = me.in_group(*steps[i])[0]
        return remote(column.at[n.zs], pieces.at[me.g], send3.at[i], recv3.at[i], device)

    for i in range(len(steps)):
        scatter(i).start()
    piece = own[me.g]
    for i in range(len(steps)):
        scatter(i).wait_recv()
        piece = piece + parts[i]
    total[...] = piece
    column[me.z] = piece
    for d in climbs:
        around(d).start()
    for d in climbs:
        around(d).wait_recv()
    piece = column[0]
    for z in range(1, n.zs):
        piece = piece + column[z]
    column[n.zs] = piece
    pieces[me.g] = piece
    for i in range(len(steps)):
        gather(i).start()
    for c in range(1, n.comps):
        for d in shares:
            share(c, d, 1).start()
    for i in range(len(steps)):
        gather(i).wait_recv()
    for i in range(n.group):
        gram[i * n.piece : (i + 1) * n.piece, :] = pieces[i]

    scale = math.sqrt(n.comps * n.vox * n.nx * n.ny)
    for k, rows in enumerate(whiten(gram[...], n.modes, scale)):
        white[8 * k : 8 * k + 8, :] = rows
    mix_t = jnp.dot(
        coef_t[...], white[...], precision=lax.Precision.HIGHEST, preferred_element_type=F32
    ).astype(BF16)

    def back(c, d):
        to = lax.rem(me.x + d, n.x)
        src = held.at[c, :, pl.ds(pl.multiple_of(to * n.own, n.own), n.own)]
        dst = out.at[c, pl.ds(me.x * n.rows, n.rows)]
        return remote(src, dst, send4.at[c, d], recv4.at[c, d], {"mode": me.zh * n.x + to})

    kept = pl.ds(pl.multiple_of(me.x * n.own, n.own), n.own)
    for c in range(n.comps):
        for d in shares:
            share(c, d, 1).wait_recv()
        for k in range(n.rows):
            held[c, k] = jnp.dot(mix_t, block[c, k], preferred_element_type=F32).astype(BF16)
        for d in range(1, n.x):
            back(c, d).start()
        out[c, pl.ds(me.x * n.rows, n.rows)] = held[c, :, kept, :]

    for c in range(n.comps):
        for r in range(3):
            for d in range(2):
                hop(r, c, d).wait_send()
        for d in shares:
            share(c, d, 0).wait_send()
            share(c, d, 1).wait_send()
    for i in range(len(steps)):
        scatter(i).wait_send()
        gather(i).wait_send()
    for d in climbs:
        around(d).wait_send()
    for c in range(n.comps):
        for d in range(1, n.x):
            back(c, d).wait()


def run(n, y0, cls, table, coef_t):
    plane = (n.comps, n.nx, n.own, n.ny)
    piece = (n.piece, n.modes)
    square = (n.modes, n.modes)
    vmem = pl.BlockSpec(memory_space=pltpu.VMEM)
    dma = lambda *shape: [pltpu.SemaphoreType.DMA(shape)] * 2
    return pl.pallas_call(
        functools.partial(kernel, n),
        out_shape=jax.ShapeDtypeStruct(plane, BF16),
        in_specs=[vmem, vmem, pl.BlockSpec(memory_space=pltpu.SMEM), vmem],
        out_specs=vmem,
        scratch_shapes=[
            pltpu.VMEM((3, 2) + plane, BF16),
            pltpu.VMEM((2, n.nx, n.ny), F32),
            pltpu.VMEM((n.nx, n.ny), F32),
        ]
        + [pltpu.VMEM((n.nx, n.own, n.ny), F32)] * 4
        + [pltpu.VMEM(plane, F32)] * 2
        + [pltpu.VMEM(plane, BF16)] * 3
        + [
            pltpu.VMEM((n.comps, n.rows, n.modes, n.ny), BF16),
            pltpu.VMEM((n.group,) + piece, F32),
            pltpu.VMEM((n.group,) + piece, F32),
            pltpu.VMEM((n.zs + 1,) + piece, F32),
            pltpu.VMEM(piece, F32),
            pltpu.VMEM((n.group,) + piece, F32),
            pltpu.VMEM(square, F32),
            pltpu.VMEM(square, F32),
            pltpu.VMEM((n.comps, n.rows, n.x * n.own, n.ny), BF16),
        ]
        + dma(3, 2, n.comps) + dma(2) + dma(2, n.comps, n.mode)
        + dma(n.group) + dma(n.zs) + dma(n.group) + dma(n.comps, n.x),
        compiler_params=pltpu.CompilerParams(
            collective_id=1, has_side_effects=True, vmem_limit_bytes=48 << 20
        ),
        name="ritz",
    )(y0, cls, table, coef_t)


def per_device(n, modes_in, class_map, stiffness_table, coefficients):
    y0 = jnp.transpose(modes_in[:, :, 0], (1, 2, 0, 3))
    width = n.x * n.own
    start = lax.div(lax.axis_index("mode"), n.x) * width
    coef_t = lax.dynamic_slice_in_dim(coefficients.T, start, width, 0)
    result = run(n, y0, class_map[0], stiffness_table, coef_t)
    return jnp.transpose(result, (2, 0, 1, 3))[:, :, None]


def build(mesh, n):
    spec = P("mode", None, "vox", None, None)
    return jax.shard_map(
        functools.partial(per_device, n), mesh=mesh,
        in_specs=(spec, P("vox", None, None), P(), P()), out_specs=spec, check_vma=False,
    )


def solution(mesh):
    return build(mesh, Sizes(y=4, z_lo=8, z_hi=2, x=4))
```

```python
import functools
import math

import jax
import jax.numpy as jnp
from jax import lax
from jax.experimental import pallas as pl
from jax.experimental.pallas import tpu as pltpu
from jax.sharding import PartitionSpec as P

MESH = pl.DeviceIdType.MESH
F32 = jnp.float32
BF16 = jnp.bfloat16
E = 21.0
CENTRE = 35.0


class Sizes:
    def __init__(self, y, z_lo, z_hi, x, own=16, comps=3, nx=32, ny=128):
        self.y, self.z_lo, self.z_hi, self.x = y, z_lo, z_hi, x
        self.vox = y * z_lo * 2
        self.mode = z_hi * x
        self.own, self.comps, self.nx, self.ny = own, comps, nx, ny
        self.modes = self.mode * own
        self.rows = nx // x
        self.half = self.rows // z_hi
        self.group = x * y * 2
        self.zs = z_hi * z_lo
        self.piece = self.modes // self.group


class Place:
    def __init__(self, n):
        self.n = n
        self.v = lax.axis_index("vox")
        self.m = lax.axis_index("mode")
        self.y = lax.div(self.v, n.z_lo * 2)
        self.zl = lax.rem(lax.div(self.v, 2), n.z_lo)
        self.c = lax.rem(self.v, 2)
        self.zh = lax.div(self.m, n.x)
        self.x = lax.rem(self.m, n.x)
        self.g = (self.x * n.y + self.y) * 2 + self.c
        self.z = self.zh * n.z_lo + self.zl

    def in_group(self, dx, dy, dc):
        n = self.n
        x, y, c = lax.rem(self.x + dx, n.x), lax.rem(self.y + dy, n.y), lax.rem(self.c + dc, 2)
        device = {"vox": (y * n.z_lo + self.zl) * 2 + c, "mode": self.zh * n.x + x}
        return device, (x * n.y + y) * 2 + c

    def in_column(self, z):
        n = self.n
        zl, zh = lax.rem(z, n.z_lo), lax.div(z, n.z_lo)
        return {"vox": (self.y * n.z_lo + zl) * 2 + self.c, "mode": zh * n.x + self.x}


def remote(src, dst, send, recv, device):
    return pltpu.make_async_remote_copy(
        src_ref=src, dst_ref=dst, send_sem=send, recv_sem=recv,
        device_id=device, device_id_type=MESH,
    )


def sum_rows(a, before, after):
    return (before + after) + (a + a)


def whiten(gram, size, scale):
    row = lax.broadcasted_iota(jnp.int32, (size, size), 0)
    rest = gram
    inverse = jnp.where(row == lax.broadcasted_iota(jnp.int32, (size, size), 1), 1.0, 0.0)
    sub = row[:8]
    done = []
    for k in range(size // 8):
        left = size - 8 * k
        wide = lambda a, i: jnp.broadcast_to(a[i : i + 1], (left, size))
        cols = [
            jnp.broadcast_to(rest[:, 8 * k + j : 8 * k + j + 1], (left, size)) for j in range(8)
        ]
        root = jnp.zeros((8, size), F32)
        for i in range(8):
            pivot = cols[i][i : i + 1]
            inv = 1.0 / pivot
            factor = jnp.where(row[:left] > i, cols[i], 0.0) * jnp.broadcast_to(inv, (left, size))
            for j in range(i + 1, 8):
                cols[j] = cols[j] - factor * wide(cols[j], i)
            rest = rest - factor * wide(rest, i)
            inverse = inverse - factor * wide(inverse, i)
            root = jnp.where(sub == i, jnp.broadcast_to(lax.rsqrt(pivot) * scale, (8, size)), root)
        done.append(inverse[:8] * root)
        rest, inverse = rest[8:], inverse[8:]
    return done


def kernel(
    n, modes_hbm, cls_hbm, table_hbm, coef_hbm, out,
    raw, cls, table, coef, loaded, mixed, y0, halo, shalo, sown, sm, sh, sp, dd, y1, y2, y1b, y2b, filt, block,
    own, parts, column, total, pieces, gram, white, held,
    hsend, hrecv, ssend, srecv, asend, arecv,
    send1, recv1, send2, recv2, send3, recv3, send4, recv4,
):
    me = Place(n)
    nxt = {"vox": lax.rem(me.v + 1, n.vox)}
    prv = {"vox": lax.rem(me.v + n.vox - 1, n.vox)}
    far = lambda d, size: min(d, size - d)
    steps = [(dx, dy, dc) for dx in range(n.x) for dy in range(n.y) for dc in range(2)]
    steps = sorted(steps[1:], key=lambda s: (-far(s[0], n.x) - far(s[1], n.y), s))
    climbs = sorted(range(1, n.zs), key=lambda d: (-far(d, n.zs), d))

    loads = [
        pltpu.make_async_copy(cls_hbm, cls, loaded.at[0]),
        pltpu.make_async_copy(table_hbm, table, loaded.at[1]),
        pltpu.make_async_copy(coef_hbm, coef, loaded.at[2]),
    ]
    loads += [
        pltpu.make_async_copy(modes_hbm.at[:, c], raw.at[:, c], loaded.at[3 + c])
        for c in range(n.comps)
    ]
    for load in loads:
        load.start()

    barrier = pltpu.get_barrier_semaphore()
    friends = [nxt, prv]
    friends += [me.in_group(*step)[0] for step in steps]
    friends += [me.in_column(lax.rem(me.z + d, n.zs)) for d in climbs]
    for dz in range(1, n.z_hi):
        for dx in range(1, n.x):
            friends.append({
                "mode": lax.rem(me.zh + dz, n.z_hi) * n.x + lax.rem(me.x + dx, n.x)
            })
    for device in friends:
        pl.semaphore_signal(barrier, inc=1, device_id=device, device_id_type=MESH)

    size = n.own * n.own
    at_row = lax.broadcasted_iota(jnp.int32, (size, size), 0)
    at_col = lax.broadcasted_iota(jnp.int32, (size, size), 1)
    swap = jnp.where(
        at_col == lax.rem(at_row, n.own) * n.own + lax.div(at_row, n.own), 1.0, 0.0
    ).astype(BF16)

    def turn(c):
        for x in range(0, n.nx, n.own):
            tile = raw[:, c, x : x + n.own, :].reshape(size, n.ny)
            turned = jnp.dot(swap, tile, preferred_element_type=F32).astype(BF16)
            y0[c, x : x + n.own] = turned.reshape(n.own, n.own, n.ny)

    for load in loads[:2]:
        load.wait()
    planes = cls[...]
    s = jnp.zeros((n.nx, n.ny), F32)
    for k in range(table.shape[0]):
        s = s + jnp.where(planes == k, table[k], 0.0)
    sown[...] = s
    for c in range(n.comps):
        loads[3 + c].wait()
        turn(c)
    loads[2].wait()
    pl.semaphore_wait(barrier, len(friends))

    scopies = [
        remote(sown, shalo.at[d], ssend.at[d], srecv.at[d], (nxt, prv)[d]) for d in range(2)
    ]
    for copy in scopies:
        copy.start()

    strip = 4
    cuts = [n.nx // 2 + strip, n.nx // 2, n.nx // 2 - strip, n.nx // 2 - 2 * strip]
    parts_of = lambda r: (slice(0, cuts[r]), slice(cuts[r], n.nx))

    def hop(r, c, d, p):
        src = (y0, y1b, y2b)[r]
        rows = parts_of(r)[p]
        at = pl.ds(rows.start, rows.stop - rows.start)
        return remote(
            src.at[c, at], halo.at[r, d, c, at],
            hsend.at[r, d, c, p], hrecv.at[r, d, c, p], (nxt, prv)[d],
        )

    for c in range(n.comps):
        for p in range(2):
            for d in range(2):
                hop(0, c, d, p).start()

    for copy in scopies:
        copy.wait()
    below, above = shalo[0], shalo[1]
    col = lax.broadcasted_iota(jnp.int32, (n.nx, n.ny), 1)
    row = lax.broadcasted_iota(jnp.int32, (n.nx, n.ny), 0)
    layers = sum_rows(s, below, above)
    ty = sum_rows(
        layers,
        jnp.where(col == 0, 0.0, pltpu.roll(layers, 1, 1)),
        jnp.where(col == n.ny - 1, 0.0, pltpu.roll(layers, n.ny - 1, 1)),
    )
    txy = sum_rows(
        ty,
        jnp.where(row == 0, 0.0, pltpu.roll(ty, 1, 0)),
        jnp.where(row == n.nx - 1, 0.0, pltpu.roll(ty, n.nx - 1, 0)),
    )
    diag = (8.0 * s + 0.125 * txy - CENTRE) * (1.0 / E)
    part = 1.0 / (8.0 * E)
    for held_in, values in ((sm, below * part), (sh, s * (2.0 * part)), (sp, above * part), (dd, diag)):
        for x in range(n.nx):
            held_in[x] = jnp.broadcast_to(values[x : x + 1, :], (n.own, n.ny))

    lane = lax.broadcasted_iota(jnp.int32, (n.own, n.ny), 1)
    first, last = lane == 0, lane == n.ny - 1

    def along_y(u):
        rows = []
        for i in range(u.shape[0]):
            v = u[i]
            before = jnp.where(first, 0.0, pltpu.roll(v, 1, 1))
            after = jnp.where(last, 0.0, pltpu.roll(v, n.ny - 1, 1))
            rows.append(sum_rows(v, before, after))
        return jnp.stack(rows)

    def stencil(r, c, arrive, leave):
        def centre(at):
            if r == 0:
                return y0[c, at].astype(F32)
            return (y1, y2)[r - 1][c, at]

        def layer_sums(lo_row, hi_row):
            at = slice(lo_row, hi_row)
            lo, mid, hi = halo[r, 0, c, at].astype(F32), centre(at), halo[r, 1, c, at].astype(F32)
            plain = (lo + hi) * 0.5 + mid
            weighted = sm[at] * lo + sh[at] * mid + sp[at] * hi
            return along_y(plain), along_y(weighted)

        zero = jnp.zeros((1, n.own, n.ny), F32)
        arrive(0)
        a, b = layer_sums(0, 1)
        a, b = jnp.concatenate([zero, a]), jnp.concatenate([zero, b])
        for x in range(0, n.nx, strip):
            at = slice(x, x + strip)
            if x + strip == cuts[r]:
                leave(0)
                arrive(1)
            more = list(layer_sums(x + 1, min(x + strip + 1, n.nx)))
            if x + strip == n.nx:
                more = [jnp.concatenate([u, zero]) for u in more]
            a, b = jnp.concatenate([a, more[0]]), jnp.concatenate([b, more[1]])
            fold = lambda u: sum_rows(u[1 : strip + 1], u[:strip], u[2:])
            value = dd[at] * centre(at) - (sh[at] * fold(a) + fold(b))
            a, b = a[strip:], b[strip:]
            if r == 0:
                y1[c, at] = value
                y1b[c, at] = value.astype(BF16)
            elif r == 1:
                value = (value + value) - y0[c, at].astype(F32)
                y2[c, at] = value
                y2b[c, at] = value.astype(BF16)
            else:
                filt[c, at] = ((value + value) - y1[c, at]).astype(BF16)
        leave(1)

    mine = pl.ds(pl.multiple_of(me.m * n.own, n.own), n.own)

    def share(c, d, part):
        to = lax.rem(me.m + d, n.mode)
        to_x, to_zh = lax.rem(to, n.x), lax.div(to, n.x)
        at = lax.rem(to_zh + part, n.z_hi) * n.half
        src = filt.at[c, pl.ds(to_x * n.rows + at, n.half)]
        dst = block.at[c, pl.ds(at, n.half), mine]
        return remote(src, dst, asend.at[part, c, d], arecv.at[part, c, d], {"mode": to})

    shares = range(1, n.mode)
    for r in range(3):
        for c in range(n.comps):
            def arrive(p):
                for d in range(2):
                    hop(r, c, d, p).wait_recv()

            def leave(p):
                if r < 2:
                    for d in range(2):
                        hop(r + 1, c, d, p).start()

            stencil(r, c, arrive, leave)
            if r == 2:
                for d in shares:
                    share(c, d, 0).start()
                block[c, :, mine, :] = filt[c, pl.ds(me.x * n.rows, n.rows)]
    for d in shares:
        share(0, d, 1).start()

    product = jnp.zeros((n.modes, n.modes), F32)
    for c in range(n.comps):
        for d in shares:
            share(c, d, 0).wait_recv()
        for k in range(n.half):
            a = block[c, me.zh * n.half + k]
            product = product + lax.dot_general(
                a, a, (((1,), (1,)), ((), ())), preferred_element_type=F32
            )
    for i in range(n.group):
        own[i] = product[i * n.piece : (i + 1) * n.piece]

    def scatter(i):
        device, to = me.in_group(*steps[i])
        return remote(own.at[to], parts.at[i], send1.at[i], recv1.at[i], device)

    def around(d):
        to = me.in_column(lax.rem(me.z + d, n.zs))
        return remote(total, column.at[me.z], send2.at[d], recv2.at[d], to)

    def gather(i):
        device = me.in_group(*steps[i])[0]
        return remote(column.at[n.zs], pieces.at[me.g], send3.at[i], recv3.at[i], device)

    for i in range(len(steps)):
        scatter(i).start()
    piece = own[me.g]
    for i in range(len(steps)):
        scatter(i).wait_recv()
        piece = piece + parts[i]
    total[...] = piece
    column[me.z] = piece
    for d in climbs:
        around(d).start()
    for d in climbs:
        around(d).wait_recv()
    piece = column[0]
    for z in range(1, n.zs):
        piece = piece + column[z]
    column[n.zs] = piece
    pieces[me.g] = piece
    for i in range(len(steps)):
        gather(i).start()
    for c in range(1, n.comps):
        for d in shares:
            share(c, d, 1).start()
    for i in range(len(steps)):
        gather(i).wait_recv()
    for i in range(n.group):
        gram[i * n.piece : (i + 1) * n.piece, :] = pieces[i]

    scale = math.sqrt(n.comps * n.vox * n.nx * n.ny)
    for k, rows in enumerate(whiten(gram[...], n.modes, scale)):
        white[8 * k : 8 * k + 8, :] = rows
    mixed[...] = lax.dot_general(
        coef[...], white[...], (((0,), (0,)), ((), ())),
        precision=lax.Precision.HIGHEST, preferred_element_type=F32,
    )
    width = n.x * n.own
    mix_t = mixed[pl.ds(pl.multiple_of(me.zh * width, width), width), :].astype(BF16)

    def back(c, d):
        to = lax.rem(me.x + d, n.x)
        src = held.at[c, :, pl.ds(pl.multiple_of(to * n.own, n.own), n.own)]
        dst = out.at[c, pl.ds(me.x * n.rows, n.rows)]
        return remote(src, dst, send4.at[c, d], recv4.at[c, d], {"mode": me.zh * n.x + to})

    kept = pl.ds(pl.multiple_of(me.x * n.own, n.own), n.own)
    for c in range(n.comps):
        for d in shares:
            share(c, d, 1).wait_recv()
        for k in range(n.rows):
            held[c, k] = jnp.dot(mix_t, block[c, k], preferred_element_type=F32).astype(BF16)
        for d in range(1, n.x):
            back(c, d).start()
        out[c, pl.ds(me.x * n.rows, n.rows)] = held[c, :, kept, :]

    for c in range(n.comps):
        for r in range(3):
            for d in range(2):
                for p in range(2):
                    hop(r, c, d, p).wait_send()
        for d in shares:
            share(c, d, 0).wait_send()
            share(c, d, 1).wait_send()
    for i in range(len(steps)):
        scatter(i).wait_send()
        gather(i).wait_send()
    for d in climbs:
        around(d).wait_send()
    for c in range(n.comps):
        for d in range(1, n.x):
            back(c, d).wait()


def run(n, modes_in, class_map, table, coefficients):
    plane = (n.comps, n.nx, n.own, n.ny)
    piece = (n.piece, n.modes)
    square = (n.modes, n.modes)
    vmem = pl.BlockSpec(memory_space=pltpu.VMEM)
    dma = lambda *shape: [pltpu.SemaphoreType.DMA(shape)] * 2
    return pl.pallas_call(
        functools.partial(kernel, n),
        out_shape=jax.ShapeDtypeStruct(plane, BF16),
        in_specs=[pl.BlockSpec(memory_space=pltpu.HBM)] * 4,
        out_specs=vmem,
        scratch_shapes=[
            pltpu.VMEM((n.own, n.comps, n.nx, n.ny), BF16),
            pltpu.VMEM((n.nx, n.ny), jnp.int32),
            pltpu.SMEM(table.shape, F32),
            pltpu.VMEM(square, F32),
            pltpu.SemaphoreType.DMA((3 + n.comps,)),
            pltpu.VMEM(square, F32),
            pltpu.VMEM(plane, BF16),
            pltpu.VMEM((3, 2) + plane, BF16),
            pltpu.VMEM((2, n.nx, n.ny), F32),
            pltpu.VMEM((n.nx, n.ny), F32),
        ]
        + [pltpu.VMEM((n.nx, n.own, n.ny), F32)] * 4
        + [pltpu.VMEM(plane, F32)] * 2
        + [pltpu.VMEM(plane, BF16)] * 3
        + [
            pltpu.VMEM((n.comps, n.rows, n.modes, n.ny), BF16),
            pltpu.VMEM((n.group,) + piece, F32),
            pltpu.VMEM((n.group,) + piece, F32),
            pltpu.VMEM((n.zs + 1,) + piece, F32),
            pltpu.VMEM(piece, F32),
            pltpu.VMEM((n.group,) + piece, F32),
            pltpu.VMEM(square, F32),
            pltpu.VMEM(square, F32),
            pltpu.VMEM((n.comps, n.rows, n.x * n.own, n.ny), BF16),
        ]
        + dma(3, 2, n.comps, 2) + dma(2) + dma(2, n.comps, n.mode)
        + dma(n.group) + dma(n.zs) + dma(n.group) + dma(n.comps, n.x),
        compiler_params=pltpu.CompilerParams(
            collective_id=1, has_side_effects=True, vmem_limit_bytes=62 << 20
        ),
        name="ritz",
    )(modes_in, class_map, table, coefficients)


def per_device(n, modes_in, class_map, stiffness_table, coefficients):
    result = run(n, modes_in[:, :, 0], class_map[0], stiffness_table, coefficients)
    return jnp.transpose(result, (2, 0, 1, 3))[:, :, None]


def build(mesh, n):
    spec = P("mode", None, "vox", None, None)
    return jax.shard_map(
        functools.partial(per_device, n), mesh=mesh,
        in_specs=(spec, P("vox", None, None), P(), P()), out_specs=spec, check_vma=False,
    )


def solution(mesh):
    return build(mesh, Sizes(y=4, z_lo=8, z_hi=2, x=4))
```

```python
import functools
import math

import jax
import jax.numpy as jnp
from jax import lax
from jax.experimental import pallas as pl
from jax.experimental.pallas import tpu as pltpu
from jax.sharding import PartitionSpec as P

MESH = pl.DeviceIdType.MESH
F32 = jnp.float32
BF16 = jnp.bfloat16
E = 21.0
CENTRE = 35.0


class Sizes:
    def __init__(self, y, z_lo, z_hi, x, own=16, comps=3, nx=32, ny=128):
        self.y, self.z_lo, self.z_hi, self.x = y, z_lo, z_hi, x
        self.vox = y * z_lo * 2
        self.mode = z_hi * x
        self.own, self.comps, self.nx, self.ny = own, comps, nx, ny
        self.modes = self.mode * own
        self.rows = nx // x
        self.half = self.rows // z_hi
        self.group = x * y * 2
        self.zs = z_hi * z_lo
        self.piece = self.modes // self.group


class Place:
    def __init__(self, n):
        self.n = n
        self.v = lax.axis_index("vox")
        self.m = lax.axis_index("mode")
        self.y = lax.div(self.v, n.z_lo * 2)
        self.zl = lax.rem(lax.div(self.v, 2), n.z_lo)
        self.c = lax.rem(self.v, 2)
        self.zh = lax.div(self.m, n.x)
        self.x = lax.rem(self.m, n.x)
        self.g = (self.x * n.y + self.y) * 2 + self.c
        self.z = self.zh * n.z_lo + self.zl

    def in_group(self, dx, dy, dc):
        n = self.n
        x, y, c = lax.rem(self.x + dx, n.x), lax.rem(self.y + dy, n.y), lax.rem(self.c + dc, 2)
        device = {"vox": (y * n.z_lo + self.zl) * 2 + c, "mode": self.zh * n.x + x}
        return device, (x * n.y + y) * 2 + c

    def in_column(self, z):
        n = self.n
        zl, zh = lax.rem(z, n.z_lo), lax.div(z, n.z_lo)
        return {"vox": (self.y * n.z_lo + zl) * 2 + self.c, "mode": zh * n.x + self.x}


def remote(src, dst, send, recv, device):
    return pltpu.make_async_remote_copy(
        src_ref=src, dst_ref=dst, send_sem=send, recv_sem=recv,
        device_id=device, device_id_type=MESH,
    )


def sum_rows(a, before, after):
    return (before + after) + (a + a)


def whiten(gram, size, scale):
    row = lax.broadcasted_iota(jnp.int32, (size, size), 0)
    rest = gram
    inverse = jnp.where(row == lax.broadcasted_iota(jnp.int32, (size, size), 1), 1.0, 0.0)
    sub = row[:8]
    done = []
    for k in range(size // 8):
        left = size - 8 * k
        wide = lambda a, i: jnp.broadcast_to(a[i : i + 1], (left, size))
        cols = [
            jnp.broadcast_to(rest[:, 8 * k + j : 8 * k + j + 1], (left, size)) for j in range(8)
        ]
        root = jnp.zeros((8, size), F32)
        for i in range(8):
            pivot = cols[i][i : i + 1]
            inv = 1.0 / pivot
            factor = jnp.where(row[:left] > i, cols[i], 0.0) * jnp.broadcast_to(inv, (left, size))
            for j in range(i + 1, 8):
                cols[j] = cols[j] - factor * wide(cols[j], i)
            rest = rest - factor * wide(rest, i)
            inverse = inverse - factor * wide(inverse, i)
            root = jnp.where(sub == i, jnp.broadcast_to(lax.rsqrt(pivot) * scale, (8, size)), root)
        done.append(inverse[:8] * root)
        rest, inverse = rest[8:], inverse[8:]
    return done


def kernel(
    n, modes_hbm, cls_hbm, table_hbm, coef_hbm, out,
    raw, cls, table, coef, loaded, mixed, y0, halo, shalo, sown, sm, sh, sp, dd, y1, y2, y1b, y2b, filt, block,
    own, parts, column, total, pieces, gram, white, held,
    hsend, hrecv, ssend, srecv, asend, arecv,
    send1, recv1, send2, recv2, send3, recv3, send4, recv4,
):
    me = Place(n)
    nxt = {"vox": lax.rem(me.v + 1, n.vox)}
    prv = {"vox": lax.rem(me.v + n.vox - 1, n.vox)}
    far = lambda d, size: min(d, size - d)
    steps = [(dx, dy, dc) for dx in range(n.x) for dy in range(n.y) for dc in range(2)]
    steps = sorted(steps[1:], key=lambda s: (-far(s[0], n.x) - far(s[1], n.y), s))
    climbs = sorted(range(1, n.zs), key=lambda d: (-far(d, n.zs), d))

    loads = [
        pltpu.make_async_copy(cls_hbm, cls, loaded.at[0]),
        pltpu.make_async_copy(table_hbm, table, loaded.at[1]),
        pltpu.make_async_copy(coef_hbm, coef, loaded.at[2]),
    ]
    loads += [
        pltpu.make_async_copy(modes_hbm.at[:, c], raw.at[:, c], loaded.at[3 + c])
        for c in range(n.comps)
    ]
    for load in loads:
        load.start()

    barrier = pltpu.get_barrier_semaphore()
    friends = [nxt, prv]
    friends += [me.in_group(*step)[0] for step in steps]
    friends += [me.in_column(lax.rem(me.z + d, n.zs)) for d in climbs]
    for dz in range(1, n.z_hi):
        for dx in range(1, n.x):
            friends.append({
                "mode": lax.rem(me.zh + dz, n.z_hi) * n.x + lax.rem(me.x + dx, n.x)
            })
    for device in friends:
        pl.semaphore_signal(barrier, inc=1, device_id=device, device_id_type=MESH)

    size = n.own * n.own
    at_row = lax.broadcasted_iota(jnp.int32, (size, size), 0)
    at_col = lax.broadcasted_iota(jnp.int32, (size, size), 1)
    swap = jnp.where(
        at_col == lax.rem(at_row, n.own) * n.own + lax.div(at_row, n.own), 1.0, 0.0
    ).astype(BF16)

    def turn(c):
        for x in range(0, n.nx, n.own):
            tile = raw[:, c, x : x + n.own, :].reshape(size, n.ny)
            turned = jnp.dot(swap, tile, preferred_element_type=F32).astype(BF16)
            y0[c, x : x + n.own] = turned.reshape(n.own, n.own, n.ny)

    for load in loads[:2]:
        load.wait()
    planes = cls[...]
    s = jnp.zeros((n.nx, n.ny), F32)
    for k in range(table.shape[0]):
        s = s + jnp.where(planes == k, table[k], 0.0)
    sown[...] = s
    for c in range(n.comps):
        loads[3 + c].wait()
        turn(c)
    loads[2].wait()
    pl.semaphore_wait(barrier, len(friends))

    scopies = [
        remote(sown, shalo.at[d], ssend.at[d], srecv.at[d], (nxt, prv)[d]) for d in range(2)
    ]
    for copy in scopies:
        copy.start()

    strip = 4
    cuts = [n.nx // 2 + strip, n.nx // 2, n.nx // 2 - strip, n.nx // 2 - 2 * strip]
    parts_of = lambda r: (slice(0, cuts[r]), slice(cuts[r], n.nx))

    def hop(r, c, d, p):
        src = (y0, y1b, y2b)[r]
        rows = parts_of(r)[p]
        at = pl.ds(rows.start, rows.stop - rows.start)
        return remote(
            src.at[c, at], halo.at[r, d, c, at],
            hsend.at[r, d, c, p], hrecv.at[r, d, c, p], (nxt, prv)[d],
        )

    for c in range(n.comps):
        for p in range(2):
            for d in range(2):
                hop(0, c, d, p).start()

    for copy in scopies:
        copy.wait()
    below, above = shalo[0], shalo[1]
    col = lax.broadcasted_iota(jnp.int32, (n.nx, n.ny), 1)
    row = lax.broadcasted_iota(jnp.int32, (n.nx, n.ny), 0)
    layers = sum_rows(s, below, above)
    ty = sum_rows(
        layers,
        jnp.where(col == 0, 0.0, pltpu.roll(layers, 1, 1)),
        jnp.where(col == n.ny - 1, 0.0, pltpu.roll(layers, n.ny - 1, 1)),
    )
    txy = sum_rows(
        ty,
        jnp.where(row == 0, 0.0, pltpu.roll(ty, 1, 0)),
        jnp.where(row == n.nx - 1, 0.0, pltpu.roll(ty, n.nx - 1, 0)),
    )
    diag = (8.0 * s + 0.125 * txy - CENTRE) * (1.0 / E)
    part = 1.0 / (8.0 * E)
    for held_in, values in ((sm, below * part), (sh, s * (2.0 * part)), (sp, above * part), (dd, diag)):
        for x in range(n.nx):
            held_in[x] = jnp.broadcast_to(values[x : x + 1, :], (n.own, n.ny))

    lane = lax.broadcasted_iota(jnp.int32, (n.own, n.ny), 1)
    first, last = lane == 0, lane == n.ny - 1

    def along_y(u):
        rows = []
        for i in range(u.shape[0]):
            v = u[i]
            before = jnp.where(first, 0.0, pltpu.roll(v, 1, 1))
            after = jnp.where(last, 0.0, pltpu.roll(v, n.ny - 1, 1))
            rows.append(sum_rows(v, before, after))
        return jnp.stack(rows)

    def stencil(r, c, arrive, leave):
        def centre(at):
            if r == 0:
                return y0[c, at].astype(F32)
            return (y1, y2)[r - 1][c, at]

        def layer_sums(lo_row, hi_row):
            at = slice(lo_row, hi_row)
            lo, mid, hi = halo[r, 0, c, at].astype(F32), centre(at), halo[r, 1, c, at].astype(F32)
            plain = (lo + hi) * 0.5 + mid
            weighted = sm[at] * lo + sh[at] * mid + sp[at] * hi
            return along_y(plain), along_y(weighted)

        zero = jnp.zeros((1, n.own, n.ny), F32)
        arrive(0)
        a, b = layer_sums(0, 1)
        a, b = jnp.concatenate([zero, a]), jnp.concatenate([zero, b])
        for x in range(0, n.nx, strip):
            at = slice(x, x + strip)
            if x + strip == cuts[r]:
                leave(0)
                arrive(1)
            more = list(layer_sums(x + 1, min(x + strip + 1, n.nx)))
            if x + strip == n.nx:
                more = [jnp.concatenate([u, zero]) for u in more]
            a, b = jnp.concatenate([a, more[0]]), jnp.concatenate([b, more[1]])
            fold = lambda u: sum_rows(u[1 : strip + 1], u[:strip], u[2:])
            value = dd[at] * centre(at) - (sh[at] * fold(a) + fold(b))
            a, b = a[strip:], b[strip:]
            if r == 0:
                y1[c, at] = value
                y1b[c, at] = value.astype(BF16)
            elif r == 1:
                value = (value + value) - y0[c, at].astype(F32)
                y2[c, at] = value
                y2b[c, at] = value.astype(BF16)
            else:
                filt[c, at] = ((value + value) - y1[c, at]).astype(BF16)
        leave(1)

    def share(c, d, part):
        dz, dx = divmod(d, n.x)
        to_zh, to_x = lax.rem(me.zh + dz, n.z_hi), lax.rem(me.x + dx, n.x)
        at, count = (0, n.rows) if dz == 0 else (lax.rem(to_zh + part, n.z_hi) * n.half, n.half)
        src = filt.at[c, pl.ds(to_x * n.rows + at, count)]
        dst = block.at[c, me.m, pl.ds(at, count)]
        to = {"mode": to_zh * n.x + to_x}
        return remote(src, dst, asend.at[part, c, d], arecv.at[part, c, d], to)

    def every_mode(c, k):
        return jnp.concatenate([block[c, i, k] for i in range(n.mode)])

    others = list(range(n.x, n.mode))
    shares = others + list(range(1, n.x))
    for r in range(3):
        for c in range(n.comps):
            def arrive(p):
                for d in range(2):
                    hop(r, c, d, p).wait_recv()

            def leave(p):
                if r < 2:
                    for d in range(2):
                        hop(r + 1, c, d, p).start()

            stencil(r, c, arrive, leave)
            if r == 2:
                for d in shares:
                    share(c, d, 0).start()
                block[c, me.m] = filt[c, pl.ds(me.x * n.rows, n.rows)]
    product = jnp.zeros((n.modes, n.modes), F32)
    for c in range(n.comps):
        for d in shares:
            share(c, d, 0).wait_recv()
        for k in range(n.half):
            a = every_mode(c, me.zh * n.half + k)
            product = product + lax.dot_general(
                a, a, (((1,), (1,)), ((), ())), preferred_element_type=F32
            )
    for i in range(n.group):
        own[i] = product[i * n.piece : (i + 1) * n.piece]

    def scatter(i):
        device, to = me.in_group(*steps[i])
        return remote(own.at[to], parts.at[i], send1.at[i], recv1.at[i], device)

    def around(d):
        to = me.in_column(lax.rem(me.z + d, n.zs))
        return remote(total, column.at[me.z], send2.at[d], recv2.at[d], to)

    def gather(i):
        device = me.in_group(*steps[i])[0]
        return remote(column.at[n.zs], pieces.at[me.g], send3.at[i], recv3.at[i], device)

    for i in range(len(steps)):
        scatter(i).start()
    for d in others:
        share(0, d, 1).start()
    piece = own[me.g]
    for i in range(len(steps)):
        scatter(i).wait_recv()
        piece = piece + parts[i]
    total[...] = piece
    column[me.z] = piece
    for d in climbs:
        around(d).start()
    for d in climbs:
        around(d).wait_recv()
    piece = column[0]
    for z in range(1, n.zs):
        piece = piece + column[z]
    column[n.zs] = piece
    pieces[me.g] = piece
    for i in range(len(steps)):
        gather(i).start()
    for c in range(1, n.comps):
        for d in others:
            share(c, d, 1).start()
    for i in range(len(steps)):
        gather(i).wait_recv()
    for i in range(n.group):
        gram[i * n.piece : (i + 1) * n.piece, :] = pieces[i]

    scale = math.sqrt(n.comps * n.vox * n.nx * n.ny)
    for k, rows in enumerate(whiten(gram[...], n.modes, scale)):
        white[8 * k : 8 * k + 8, :] = rows
    mixed[...] = lax.dot_general(
        coef[...], white[...], (((0,), (0,)), ((), ())),
        precision=lax.Precision.HIGHEST, preferred_element_type=F32,
    )
    width = n.x * n.own
    mix_t = mixed[pl.ds(pl.multiple_of(me.zh * width, width), width), :].astype(BF16)

    def back(c, d):
        to = lax.rem(me.x + d, n.x)
        src = held.at[c, to]
        dst = out.at[c, pl.ds(me.x * n.rows, n.rows)]
        return remote(src, dst, send4.at[c, d], recv4.at[c, d], {"mode": me.zh * n.x + to})

    for c in range(n.comps):
        for d in others:
            share(c, d, 1).wait_recv()
        for k in range(n.rows):
            turned = jnp.dot(mix_t, every_mode(c, k), preferred_element_type=F32).astype(BF16)
            for q in range(n.x):
                held[c, q, k] = turned[q * n.own : (q + 1) * n.own]
        for d in range(1, n.x):
            back(c, d).start()
        out[c, pl.ds(me.x * n.rows, n.rows)] = held[c, me.x]

    for c in range(n.comps):
        for r in range(3):
            for d in range(2):
                for p in range(2):
                    hop(r, c, d, p).wait_send()
        for d in shares:
            share(c, d, 0).wait_send()
        for d in others:
            share(c, d, 1).wait_send()
    for i in range(len(steps)):
        scatter(i).wait_send()
        gather(i).wait_send()
    for d in climbs:
        around(d).wait_send()
    for c in range(n.comps):
        for d in range(1, n.x):
            back(c, d).wait()


def run(n, modes_in, class_map, table, coefficients):
    plane = (n.comps, n.nx, n.own, n.ny)
    piece = (n.piece, n.modes)
    square = (n.modes, n.modes)
    vmem = pl.BlockSpec(memory_space=pltpu.VMEM)
    dma = lambda *shape: [pltpu.SemaphoreType.DMA(shape)] * 2
    return pl.pallas_call(
        functools.partial(kernel, n),
        out_shape=jax.ShapeDtypeStruct(plane, BF16),
        in_specs=[pl.BlockSpec(memory_space=pltpu.HBM)] * 4,
        out_specs=vmem,
        scratch_shapes=[
            pltpu.VMEM((n.own, n.comps, n.nx, n.ny), BF16),
            pltpu.VMEM((n.nx, n.ny), jnp.int32),
            pltpu.SMEM(table.shape, F32),
            pltpu.VMEM(square, F32),
            pltpu.SemaphoreType.DMA((3 + n.comps,)),
            pltpu.VMEM(square, F32),
            pltpu.VMEM(plane, BF16),
            pltpu.VMEM((3, 2) + plane, BF16),
            pltpu.VMEM((2, n.nx, n.ny), F32),
            pltpu.VMEM((n.nx, n.ny), F32),
        ]
        + [pltpu.VMEM((n.nx, n.own, n.ny), F32)] * 4
        + [pltpu.VMEM(plane, F32)] * 2
        + [pltpu.VMEM(plane, BF16)] * 3
        + [
            pltpu.VMEM((n.comps, n.mode, n.rows, n.own, n.ny), BF16),
            pltpu.VMEM((n.group,) + piece, F32),
            pltpu.VMEM((n.group,) + piece, F32),
            pltpu.VMEM((n.zs + 1,) + piece, F32),
            pltpu.VMEM(piece, F32),
            pltpu.VMEM((n.group,) + piece, F32),
            pltpu.VMEM(square, F32),
            pltpu.VMEM(square, F32),
            pltpu.VMEM((n.comps, n.x, n.rows, n.own, n.ny), BF16),
        ]
        + dma(3, 2, n.comps, 2) + dma(2) + dma(2, n.comps, n.mode)
        + dma(n.group) + dma(n.zs) + dma(n.group) + dma(n.comps, n.x),
        compiler_params=pltpu.CompilerParams(
            collective_id=1, has_side_effects=True, vmem_limit_bytes=62 << 20
        ),
        name="ritz",
    )(modes_in, class_map, table, coefficients)


def per_device(n, modes_in, class_map, stiffness_table, coefficients):
    result = run(n, modes_in[:, :, 0], class_map[0], stiffness_table, coefficients)
    return jnp.transpose(result, (2, 0, 1, 3))[:, :, None]


def build(mesh, n):
    spec = P("mode", None, "vox", None, None)
    return jax.shard_map(
        functools.partial(per_device, n), mesh=mesh,
        in_specs=(spec, P("vox", None, None), P(), P()), out_specs=spec, check_vma=False,
    )


def solution(mesh):
    return build(mesh, Sizes(y=4, z_lo=8, z_hi=2, x=4))
```

```python
import functools
import math

import jax
import jax.numpy as jnp
from jax import lax
from jax.experimental import pallas as pl
from jax.experimental.pallas import tpu as pltpu
from jax.sharding import PartitionSpec as P

MESH = pl.DeviceIdType.MESH
F32 = jnp.float32
BF16 = jnp.bfloat16
E = 21.0
CENTRE = 35.0


class Sizes:
    def __init__(self, y, z_lo, z_hi, x, own=16, comps=3, nx=32, ny=128):
        self.y, self.z_lo, self.z_hi, self.x = y, z_lo, z_hi, x
        self.vox = y * z_lo * 2
        self.mode = z_hi * x
        self.own, self.comps, self.nx, self.ny = own, comps, nx, ny
        self.modes = self.mode * own
        self.rows = nx // x
        self.half = self.rows // z_hi
        self.group = x * y * 2
        self.zs = z_hi * z_lo
        self.piece = self.modes // self.group


class Place:
    def __init__(self, n):
        self.n = n
        self.v = lax.axis_index("vox")
        self.m = lax.axis_index("mode")
        self.y = lax.div(self.v, n.z_lo * 2)
        self.zl = lax.rem(lax.div(self.v, 2), n.z_lo)
        self.c = lax.rem(self.v, 2)
        self.zh = lax.div(self.m, n.x)
        self.x = lax.rem(self.m, n.x)
        self.g = (self.x * n.y + self.y) * 2 + self.c
        self.z = self.zh * n.z_lo + self.zl

    def in_group(self, dx, dy, dc):
        n = self.n
        x, y, c = lax.rem(self.x + dx, n.x), lax.rem(self.y + dy, n.y), lax.rem(self.c + dc, 2)
        device = {"vox": (y * n.z_lo + self.zl) * 2 + c, "mode": self.zh * n.x + x}
        return device, (x * n.y + y) * 2 + c

    def in_column(self, z):
        n = self.n
        zl, zh = lax.rem(z, n.z_lo), lax.div(z, n.z_lo)
        return {"vox": (self.y * n.z_lo + zl) * 2 + self.c, "mode": zh * n.x + self.x}


def remote(src, dst, send, recv, device):
    return pltpu.make_async_remote_copy(
        src_ref=src, dst_ref=dst, send_sem=send, recv_sem=recv,
        device_id=device, device_id_type=MESH,
    )


def sum_rows(a, before, after):
    return (before + after) + (a + a)


def whiten(gram, size, scale):
    row = lax.broadcasted_iota(jnp.int32, (size, size), 0)
    rest = gram
    inverse = jnp.where(row == lax.broadcasted_iota(jnp.int32, (size, size), 1), 1.0, 0.0)
    sub = row[:8]
    done = []
    for k in range(size // 8):
        left = size - 8 * k
        wide = lambda a, i: jnp.broadcast_to(a[i : i + 1], (left, size))
        cols = [
            jnp.broadcast_to(rest[:, 8 * k + j : 8 * k + j + 1], (left, size)) for j in range(8)
        ]
        root = jnp.zeros((8, size), F32)
        for i in range(8):
            pivot = cols[i][i : i + 1]
            inv = 1.0 / pivot
            factor = jnp.where(row[:left] > i, cols[i], 0.0) * jnp.broadcast_to(inv, (left, size))
            for j in range(i + 1, 8):
                cols[j] = cols[j] - factor * wide(cols[j], i)
            rest = rest - factor * wide(rest, i)
            inverse = inverse - factor * wide(inverse, i)
            root = jnp.where(sub == i, jnp.broadcast_to(lax.rsqrt(pivot) * scale, (8, size)), root)
        done.append(inverse[:8] * root)
        rest, inverse = rest[8:], inverse[8:]
    return done


def kernel(
    n, modes_hbm, cls_hbm, table_hbm, coef_hbm, out,
    raw, cls, table, coef, loaded, mixed, y0, halo, shalo, sown, sm, sh, sp, dd, y1, y2, y1b, y2b, filt, block,
    own, parts, column, total, pieces, gram, white, held,
    hsend, hrecv, ssend, srecv, asend, arecv,
    send1, recv1, send2, recv2, send3, recv3, send4, recv4,
):
    me = Place(n)
    nxt = {"vox": lax.rem(me.v + 1, n.vox)}
    prv = {"vox": lax.rem(me.v + n.vox - 1, n.vox)}
    far = lambda d, size: min(d, size - d)
    steps = [(dx, dy, dc) for dx in range(n.x) for dy in range(n.y) for dc in range(2)]
    steps = sorted(steps[1:], key=lambda s: (-far(s[0], n.x) - far(s[1], n.y), s))
    climbs = sorted(range(1, n.zs), key=lambda d: (-far(d, n.zs), d))

    barrier = pltpu.get_barrier_semaphore()
    friends = [nxt, prv]
    friends += [me.in_column(lax.rem(me.z + d, n.zs)) for d in climbs]
    for dz in range(1, n.z_hi):
        for dx in range(1, n.x):
            friends.append({
                "mode": lax.rem(me.zh + dz, n.z_hi) * n.x + lax.rem(me.x + dx, n.x)
            })
    friends += [me.in_group(*step)[0] for step in steps]
    for device in friends:
        pl.semaphore_signal(barrier, inc=1, device_id=device, device_id_type=MESH)

    loads = [
        pltpu.make_async_copy(cls_hbm, cls, loaded.at[0]),
        pltpu.make_async_copy(table_hbm, table, loaded.at[1]),
        pltpu.make_async_copy(coef_hbm, coef, loaded.at[2]),
    ]
    loads += [
        pltpu.make_async_copy(modes_hbm.at[:, c], raw.at[:, c], loaded.at[3 + c])
        for c in range(n.comps)
    ]
    for load in loads:
        load.start()

    size = n.own * n.own
    at_row = lax.broadcasted_iota(jnp.int32, (size, size), 0)
    at_col = lax.broadcasted_iota(jnp.int32, (size, size), 1)
    swap = jnp.where(
        at_col == lax.rem(at_row, n.own) * n.own + lax.div(at_row, n.own), 1.0, 0.0
    ).astype(BF16)

    def turn(c):
        for x in range(0, n.nx, n.own):
            tile = raw[:, c, x : x + n.own, :].reshape(size, n.ny)
            turned = jnp.dot(swap, tile, preferred_element_type=F32).astype(BF16)
            y0[c, x : x + n.own] = turned.reshape(n.own, n.own, n.ny)

    for load in loads[:2]:
        load.wait()
    planes = cls[...]
    s = jnp.zeros((n.nx, n.ny), F32)
    for k in range(table.shape[0]):
        s = s + jnp.where(planes == k, table[k], 0.0)
    sown[...] = s
    for c in range(n.comps):
        loads[3 + c].wait()
        turn(c)
    loads[2].wait()
    pl.semaphore_wait(barrier, len(friends))

    scopies = [
        remote(sown, shalo.at[d], ssend.at[d], srecv.at[d], (nxt, prv)[d]) for d in range(2)
    ]
    for copy in scopies:
        copy.start()

    strip = 4
    cuts = [n.nx // 2 + strip, n.nx // 2, n.nx // 2 - strip, n.nx // 2 - 2 * strip]
    parts_of = lambda r: (slice(0, cuts[r]), slice(cuts[r], n.nx))

    def hop(r, c, d, p):
        src = (y0, y1b, y2b)[r]
        rows = parts_of(r)[p]
        at = pl.ds(rows.start, rows.stop - rows.start)
        return remote(
            src.at[c, at], halo.at[r, d, c, at],
            hsend.at[r, d, c, p], hrecv.at[r, d, c, p], (nxt, prv)[d],
        )

    for c in range(n.comps):
        for p in range(2):
            for d in range(2):
                hop(0, c, d, p).start()

    for copy in scopies:
        copy.wait()
    below, above = shalo[0], shalo[1]
    col = lax.broadcasted_iota(jnp.int32, (n.nx, n.ny), 1)
    row = lax.broadcasted_iota(jnp.int32, (n.nx, n.ny), 0)
    layers = sum_rows(s, below, above)
    ty = sum_rows(
        layers,
        jnp.where(col == 0, 0.0, pltpu.roll(layers, 1, 1)),
        jnp.where(col == n.ny - 1, 0.0, pltpu.roll(layers, n.ny - 1, 1)),
    )
    txy = sum_rows(
        ty,
        jnp.where(row == 0, 0.0, pltpu.roll(ty, 1, 0)),
        jnp.where(row == n.nx - 1, 0.0, pltpu.roll(ty, n.nx - 1, 0)),
    )
    diag = (8.0 * s + 0.125 * txy - CENTRE) * (1.0 / E)
    part = 1.0 / (8.0 * E)
    for held_in, values in ((sm, below * part), (sh, s * (2.0 * part)), (sp, above * part), (dd, diag)):
        for x in range(n.nx):
            held_in[x] = jnp.broadcast_to(values[x : x + 1, :], (n.own, n.ny))

    lane = lax.broadcasted_iota(jnp.int32, (n.own, n.ny), 1)
    first, last = lane == 0, lane == n.ny - 1

    def along_y(u):
        rows = []
        for i in range(u.shape[0]):
            v = u[i]
            before = jnp.where(first, 0.0, pltpu.roll(v, 1, 1))
            after = jnp.where(last, 0.0, pltpu.roll(v, n.ny - 1, 1))
            rows.append(sum_rows(v, before, after))
        return jnp.stack(rows)

    def stencil(r, c, arrive, leave):
        def centre(at):
            if r == 0:
                return y0[c, at].astype(F32)
            return (y1, y2)[r - 1][c, at]

        def layer_sums(lo_row, hi_row):
            at = slice(lo_row, hi_row)
            lo, mid, hi = halo[r, 0, c, at].astype(F32), centre(at), halo[r, 1, c, at].astype(F32)
            plain = (lo + hi) * 0.5 + mid
            weighted = sm[at] * lo + sh[at] * mid + sp[at] * hi
            return along_y(plain), along_y(weighted)

        zero = jnp.zeros((1, n.own, n.ny), F32)
        arrive(0)
        a, b = layer_sums(0, 1)
        a, b = jnp.concatenate([zero, a]), jnp.concatenate([zero, b])
        for x in range(0, n.nx, strip):
            at = slice(x, x + strip)
            if x + strip == cuts[r]:
                leave(0)
                arrive(1)
            more = list(layer_sums(x + 1, min(x + strip + 1, n.nx)))
            if x + strip == n.nx:
                more = [jnp.concatenate([u, zero]) for u in more]
            a, b = jnp.concatenate([a, more[0]]), jnp.concatenate([b, more[1]])
            fold = lambda u: sum_rows(u[1 : strip + 1], u[:strip], u[2:])
            value = dd[at] * centre(at) - (sh[at] * fold(a) + fold(b))
            a, b = a[strip:], b[strip:]
            if r == 0:
                y1[c, at] = value
                y1b[c, at] = value.astype(BF16)
            elif r == 1:
                value = (value + value) - y0[c, at].astype(F32)
                y2[c, at] = value
                y2b[c, at] = value.astype(BF16)
            else:
                filt[c, at] = ((value + value) - y1[c, at]).astype(BF16)
        leave(1)

    def share(c, d, part):
        dz, dx = divmod(d, n.x)
        to_zh, to_x = lax.rem(me.zh + dz, n.z_hi), lax.rem(me.x + dx, n.x)
        at, count = (0, n.rows) if dz == 0 else (lax.rem(to_zh + part, n.z_hi) * n.half, n.half)
        src = filt.at[c, pl.ds(to_x * n.rows + at, count)]
        dst = block.at[c, me.m, pl.ds(at, count)]
        to = {"mode": to_zh * n.x + to_x}
        return remote(src, dst, asend.at[part, c, d], arecv.at[part, c, d], to)

    def every_mode(c, k):
        return jnp.concatenate([block[c, i, k] for i in range(n.mode)])

    others = list(range(n.x, n.mode))
    shares = others + list(range(1, n.x))
    for r in range(3):
        for c in range(n.comps):
            def arrive(p):
                for d in range(2):
                    hop(r, c, d, p).wait_recv()

            def leave(p):
                if r < 2:
                    for d in range(2):
                        hop(r + 1, c, d, p).start()

            stencil(r, c, arrive, leave)
            if r == 2:
                for d in shares:
                    share(c, d, 0).start()
                block[c, me.m] = filt[c, pl.ds(me.x * n.rows, n.rows)]
    product = jnp.zeros((n.modes, n.modes), F32)
    for c in range(n.comps):
        for d in shares:
            share(c, d, 0).wait_recv()
        for k in range(n.half):
            a = every_mode(c, me.zh * n.half + k)
            product = product + lax.dot_general(
                a, a, (((1,), (1,)), ((), ())), preferred_element_type=F32
            )
    for i in range(n.group):
        own[i] = product[i * n.piece : (i + 1) * n.piece]

    def scatter(i):
        device, to = me.in_group(*steps[i])
        return remote(own.at[to], parts.at[i], send1.at[i], recv1.at[i], device)

    def around(d):
        to = me.in_column(lax.rem(me.z + d, n.zs))
        return remote(total, column.at[me.z], send2.at[d], recv2.at[d], to)

    def gather(i):
        device = me.in_group(*steps[i])[0]
        return remote(column.at[n.zs], pieces.at[me.g], send3.at[i], recv3.at[i], device)

    for i in range(len(steps)):
        scatter(i).start()
    for d in others:
        share(0, d, 1).start()
    piece = own[me.g]
    for i in range(len(steps)):
        scatter(i).wait_recv()
        piece = piece + parts[i]
    total[...] = piece
    column[me.z] = piece
    for d in climbs:
        around(d).start()
    for d in climbs:
        around(d).wait_recv()
    piece = column[0]
    for z in range(1, n.zs):
        piece = piece + column[z]
    column[n.zs] = piece
    pieces[me.g] = piece
    for i in range(len(steps)):
        gather(i).start()
    for c in range(1, n.comps):
        for d in others:
            share(c, d, 1).start()
    for i in range(len(steps)):
        gather(i).wait_recv()
    for i in range(n.group):
        gram[i * n.piece : (i + 1) * n.piece, :] = pieces[i]

    scale = math.sqrt(n.comps * n.vox * n.nx * n.ny)
    for k, rows in enumerate(whiten(gram[...], n.modes, scale)):
        white[8 * k : 8 * k + 8, :] = rows
    mixed[...] = lax.dot_general(
        coef[...], white[...], (((0,), (0,)), ((), ())),
        precision=lax.Precision.HIGHEST, preferred_element_type=F32,
    )
    width = n.x * n.own
    mix_t = mixed[pl.ds(pl.multiple_of(me.zh * width, width), width), :].astype(BF16)

    def back(c, d):
        to = lax.rem(me.x + d, n.x)
        src = held.at[c, to]
        dst = out.at[c, pl.ds(me.x * n.rows, n.rows)]
        return remote(src, dst, send4.at[c, d], recv4.at[c, d], {"mode": me.zh * n.x + to})

    for c in range(n.comps):
        for d in others:
            share(c, d, 1).wait_recv()
        for k in range(n.rows):
            turned = jnp.dot(mix_t, every_mode(c, k), preferred_element_type=F32).astype(BF16)
            for q in range(n.x):
                held[c, q, k] = turned[q * n.own : (q + 1) * n.own]
        for d in range(1, n.x):
            back(c, d).start()
        out[c, pl.ds(me.x * n.rows, n.rows)] = held[c, me.x]

    for c in range(n.comps):
        for r in range(3):
            for d in range(2):
                for p in range(2):
                    hop(r, c, d, p).wait_send()
        for d in shares:
            share(c, d, 0).wait_send()
        for d in others:
            share(c, d, 1).wait_send()
    for i in range(len(steps)):
        scatter(i).wait_send()
        gather(i).wait_send()
    for d in climbs:
        around(d).wait_send()
    for c in range(n.comps):
        for d in range(1, n.x):
            back(c, d).wait()


def run(n, modes_in, class_map, table, coefficients):
    plane = (n.comps, n.nx, n.own, n.ny)
    piece = (n.piece, n.modes)
    square = (n.modes, n.modes)
    vmem = pl.BlockSpec(memory_space=pltpu.VMEM)
    dma = lambda *shape: [pltpu.SemaphoreType.DMA(shape)] * 2
    return pl.pallas_call(
        functools.partial(kernel, n),
        out_shape=jax.ShapeDtypeStruct(plane, BF16),
        in_specs=[pl.BlockSpec(memory_space=pltpu.HBM)] * 4,
        out_specs=vmem,
        scratch_shapes=[
            pltpu.VMEM((n.own, n.comps, n.nx, n.ny), BF16),
            pltpu.VMEM((n.nx, n.ny), jnp.int32),
            pltpu.SMEM(table.shape, F32),
            pltpu.VMEM(square, F32),
            pltpu.SemaphoreType.DMA((3 + n.comps,)),
            pltpu.VMEM(square, F32),
            pltpu.VMEM(plane, BF16),
            pltpu.VMEM((3, 2) + plane, BF16),
            pltpu.VMEM((2, n.nx, n.ny), F32),
            pltpu.VMEM((n.nx, n.ny), F32),
        ]
        + [pltpu.VMEM((n.nx, n.own, n.ny), F32)] * 4
        + [pltpu.VMEM(plane, F32)] * 2
        + [pltpu.VMEM(plane, BF16)] * 3
        + [
            pltpu.VMEM((n.comps, n.mode, n.rows, n.own, n.ny), BF16),
            pltpu.VMEM((n.group,) + piece, F32),
            pltpu.VMEM((n.group,) + piece, F32),
            pltpu.VMEM((n.zs + 1,) + piece, F32),
            pltpu.VMEM(piece, F32),
            pltpu.VMEM((n.group,) + piece, F32),
            pltpu.VMEM(square, F32),
            pltpu.VMEM(square, F32),
            pltpu.VMEM((n.comps, n.x, n.rows, n.own, n.ny), BF16),
        ]
        + dma(3, 2, n.comps, 2) + dma(2) + dma(2, n.comps, n.mode)
        + dma(n.group) + dma(n.zs) + dma(n.group) + dma(n.comps, n.x),
        compiler_params=pltpu.CompilerParams(
            collective_id=1, has_side_effects=True, vmem_limit_bytes=62 << 20
        ),
        name="ritz",
    )(modes_in, class_map, table, coefficients)


def per_device(n, modes_in, class_map, stiffness_table, coefficients):
    result = run(n, modes_in[:, :, 0], class_map[0], stiffness_table, coefficients)
    return jnp.transpose(result, (2, 0, 1, 3))[:, :, None]


def build(mesh, n):
    spec = P("mode", None, "vox", None, None)
    return jax.shard_map(
        functools.partial(per_device, n), mesh=mesh,
        in_specs=(spec, P("vox", None, None), P(), P()), out_specs=spec, check_vma=False,
    )


def solution(mesh):
    return build(mesh, Sizes(y=4, z_lo=8, z_hi=2, x=4))
```
